32 devices in a mesh: dp: 8 (over z, y), seq: 4 (over x, core).
Axes of the slice: x: 2, y: 2, z: 4, core: 2. Of those that a mesh axis runs over, the one named last changes fastest.
Arguments:
- hidden: bfloat16 [8, 512, 4096], P('dp', 'seq'), may hold values from -6 to 6
- query_states: bfloat16 [8, 512, 4096], P('dp', 'seq'), may hold values from -8 to 8
- saved_key_states: bfloat16 [8, 512, 256], P('dp', 'seq'), may hold values from -8 to 8
- saved_value_states: bfloat16 [8, 512, 256], P('dp', 'seq'), may hold values from -6 to 6
- out_grad: bfloat16 [8, 512, 4096], P('dp', 'seq'), may hold values from -6 to 6
- seg_lengths: int32 [8, 8], P('dp'), may hold values from 1 to 256, 512 in all within a row
- weights: float32 [4096, 512], P(('dp', 'seq')), may hold values from -4 to 4
Outputs:
- query_grad: bfloat16 [8, 512, 4096], P('dp', 'seq')
- updated: bfloat16 [4096, 512], P('dp')
The draws below stay inside these ranges and needn't reach their ends.
Inputs may be any that keep to these rules, and one draw needn't show every extreme that they name: `seg_lengths`: each trajectory's 8 lengths sum to 512; in every trajectory the longest document has exactly 256 tokens.
All inputs are finite; a program needn't handle non-finite values.
Results may differ from the reference program's by a relative error of at most 0.0072.
Values may be sent and summed in bfloat16 or wider, within the bound.
A program may use at most 128 MiB of HBM per device.

```python
import math
import jax
import jax.numpy as jnp
import numpy as np
from jax import lax

MODEL_WIDTH = 4096
QUERY_HEADS = 32
KEY_VALUE_HEADS = 2
HEAD_SIZE = 128
NSEG = 8
TRAJECTORY_TOKENS = 512
TRAJECTORY_COUNT = 8
N_DP = 8


def drawn_pair(key):
    query_seed = jax.random.fold_in(key, 101)
    key_random_seed = jax.random.fold_in(key, 202)
    query_rows = jax.random.normal(query_seed, (N_DP, TRAJECTORY_TOKENS, QUERY_HEADS, HEAD_SIZE), jnp.float32)
    keyed_values = jax.random.normal(key_random_seed, (N_DP, TRAJECTORY_TOKENS, KEY_VALUE_HEADS, HEAD_SIZE), jnp.float32)
    return (jnp.clip(query_rows, -8.0, 8.0), jnp.clip(keyed_values, -8.0, 8.0))


def draw_query_states(key, part):
    query_rows, keyed_values = drawn_pair(key)
    return query_rows.reshape(N_DP, TRAJECTORY_TOKENS, QUERY_HEADS * HEAD_SIZE).astype(jnp.bfloat16)


def draw_saved_key_states(key, part):
    query_rows, keyed_values = drawn_pair(key)
    return keyed_values.reshape(N_DP, TRAJECTORY_TOKENS, KEY_VALUE_HEADS * HEAD_SIZE).astype(jnp.bfloat16)


def with_spikes(array, rng, source, target, parts, factor):
    owner, partner = [(jnp.arange(array.shape[axis_at]) // (array.shape[axis_at] // parts)).reshape([-1 if axis == axis_at else 1 for axis in range(array.ndim)]) for axis_at in (source, target)]
    chosen = jax.random.permutation(rng, parts)[partner]
    strong = (owner == chosen) | (owner == (partner + parts // 2) % parts)
    return jnp.where(strong, factor * array, array)


def steps_of(stream_key, shape, pieces, least, largest):
    def one(position, shards_of):
        draws = jax.random.uniform(jax.random.fold_in(jax.random.fold_in(stream_key, 6), position), (shards_of,), jnp.float32, least / len(pieces), largest / len(pieces))
        return jnp.repeat(jnp.exp(draws), shape[position] // shards_of).reshape((-1,) + (1,) * (len(shape) - position - 1))

    gain = one(*pieces[0])
    for cut in pieces[1:]:
        gain = gain * one(*cut)
    return gain


def split_up(amount, total, bound, lean):
    weights = [(1 << 20) // math.isqrt(grade ** lean) + 1 for grade in range(2, amount + 1)]
    surplus, holding = total - bound - (amount - 1), [1] * (amount - 1)
    while surplus > 0:
        free = [i for i in range(amount - 1) if holding[i] < bound]
        pool, remaining = sum([weights[i] for i in free]), surplus
        for i in free:
            addition = min(bound - holding[i], max(1, remaining * weights[i] // pool), surplus)
            holding[i] = holding[i] + addition
            surplus = surplus - addition
    return np.array([bound] + holding)


def uneven_parts(own_key, count, total, bound, lean):
    if count == 2:
        one = jax.random.randint(own_key, (), max(1, total - bound), min(bound, total - 1) + 1)
        return jnp.stack([one, total - one])
    sizes = jnp.asarray(split_up(count, total, bound, lean), jnp.int32)
    twos = (count - 1) // 2
    source_of, sink = sizes[1:1 + 2 * twos:2], sizes[2:2 + 2 * twos:2]
    margin = jnp.minimum(source_of - 1, bound - sink)
    moved = jax.random.randint(jax.random.fold_in(own_key, 1), (twos,), 0, 1 << 20) % (margin + 1)
    sizes = sizes.at[1:1 + 2 * twos:2].set(source_of - moved).at[2:2 + 2 * twos:2].set(sink + moved)
    return sizes[jax.random.permutation(jax.random.fold_in(own_key, 2), count)]


def gaussian(key, extent, deviation, bound, cuts=(), held_as=jnp.bfloat16):
    result = jax.random.normal(key, extent, jnp.float32) * deviation
    if len(cuts) > 0:
        result = steps_of(key, extent, cuts, -0.22, 0.18) * result
    return jnp.clip(result, min=-bound, max=bound).astype(held_as)


def noise_with(key, dims, width, most, shards, heavy, held_as=jnp.bfloat16):
    values = width * jax.random.normal(key, dims, jnp.float32)
    if shards:
        values = values * steps_of(key, dims, shards, -0.22, 0.18)
    return jnp.clip(with_spikes(values, jax.random.fold_in(key, 3), *heavy), -most, most).astype(held_as)


def setup_inputs(seed: int = 0) -> dict:
    keys = jax.random.split(jax.random.key(seed), 8)
    return {
        "hidden": noise_with(keys[0], (TRAJECTORY_COUNT, TRAJECTORY_TOKENS, MODEL_WIDTH), 1.0, 6.0, ((0, 8), (1, 4)), (1, 2, 4, 2.0)),
        "query_states": draw_query_states(jax.random.fold_in(keys[7], 71), 0),
        "saved_key_states": draw_saved_key_states(jax.random.fold_in(keys[7], 71), 0),
        "saved_value_states": gaussian(keys[3], (TRAJECTORY_COUNT, TRAJECTORY_TOKENS, KEY_VALUE_HEADS * HEAD_SIZE), 1.0, 6.0, ((0, 8), (1, 4))),
        "out_grad": gaussian(keys[4], (TRAJECTORY_COUNT, TRAJECTORY_TOKENS, QUERY_HEADS * HEAD_SIZE), 1.0, 6.0, ((0, 8), (1, 4))),
        "seg_lengths": jax.vmap(lambda own: uneven_parts(own, NSEG, TRAJECTORY_TOKENS, TRAJECTORY_TOKENS // 2, 2))(jax.random.split(keys[5], TRAJECTORY_COUNT)).reshape((TRAJECTORY_COUNT, NSEG)).astype(jnp.int32),
        "weights": gaussian(keys[6], (MODEL_WIDTH, 2 * KEY_VALUE_HEADS * HEAD_SIZE), 1.0, 4.0, ((0, 32),), jnp.float32),
    }


learn_rate = 0.5
decay_rate = 0.1

def document_ids(lengths_row, seq_len):
    doc_ends = jnp.cumsum(lengths_row)
    positions = jnp.arange(seq_len, dtype=jnp.int32)
    return lax.optimization_barrier(jnp.sum((positions[:, None] >= doc_ends[None, :]).astype(jnp.int32), axis=1))

def head_grads(query_head, key_head, value_head, grad_head, documents):
    seq_len = query_head.shape[0]
    block_rows = min(512, seq_len)
    score_scale = query_head.shape[1] ** (-0.5)
    positions = jnp.arange(seq_len, dtype=jnp.int32)

    def one_block(running, block_index):
        key_grad, value_grad = running
        first_row = (block_index * block_rows).astype(jnp.int32)
        query_block = lax.dynamic_slice_in_dim(query_head, first_row, block_rows, 0)
        grad_block = lax.dynamic_slice_in_dim(grad_head, first_row, block_rows, 0)
        query_docs = lax.dynamic_slice_in_dim(documents, first_row, block_rows, 0)
        query_pos = first_row + jnp.arange(block_rows, dtype=jnp.int32)
        allowed = (positions[None, :] <= query_pos[:, None]) & (documents[None, :] == query_docs[:, None])
        scores = jnp.dot(query_block, key_head.T, preferred_element_type=jnp.float32) * score_scale
        scores = jnp.where(allowed, scores, -1e+30)
        shifted = jnp.exp(scores - lax.optimization_barrier(jnp.max(scores, axis=1, keepdims=True)))
        attend = shifted / lax.optimization_barrier(jnp.sum(shifted, axis=1, keepdims=True))
        prob_grad = jnp.dot(grad_block, value_head.T, preferred_element_type=jnp.float32)
        row_delta = lax.optimization_barrier(jnp.sum(attend * prob_grad, axis=1, keepdims=True))
        score_grad = (attend * (prob_grad - row_delta)).astype(jnp.bfloat16)
        query_grad = (jnp.dot(score_grad, key_head, preferred_element_type=jnp.float32) * score_scale).astype(jnp.bfloat16)
        key_grad = key_grad + jnp.dot(score_grad.T, query_block, preferred_element_type=jnp.float32) * score_scale
        value_grad = value_grad + jnp.dot(attend.astype(jnp.bfloat16).T, grad_block, preferred_element_type=jnp.float32)
        return ((key_grad, value_grad), query_grad)
    empty_grad = jnp.zeros(key_head.shape, jnp.float32)
    sums, query_grads = lax.scan(one_block, (empty_grad, empty_grad), jnp.arange(seq_len // block_rows, dtype=jnp.int32))
    return (query_grads.reshape(seq_len, query_head.shape[1]), sums[0], sums[1])

def reference(hidden, query_states, saved_key_states, saved_value_states, out_grad, seg_lengths, weights):
    query_group_size = QUERY_HEADS // KEY_VALUE_HEADS

    def trajectory(running, inputs):
        hidden_row, query_row, key_token_row, value_token_row, grad_row, lengths_row = inputs
        documents = document_ids(lengths_row, TRAJECTORY_TOKENS)
        query_heads = query_row.reshape(TRAJECTORY_TOKENS, QUERY_HEADS, HEAD_SIZE).transpose(1, 0, 2)
        grad_heads = grad_row.reshape(TRAJECTORY_TOKENS, QUERY_HEADS, HEAD_SIZE).transpose(1, 0, 2)
        key_head_states = jnp.repeat(key_token_row.reshape(TRAJECTORY_TOKENS, KEY_VALUE_HEADS, HEAD_SIZE).transpose(1, 0, 2), query_group_size, axis=0)
        value_head_states = jnp.repeat(value_token_row.reshape(TRAJECTORY_TOKENS, KEY_VALUE_HEADS, HEAD_SIZE).transpose(1, 0, 2), query_group_size, axis=0)

        def per_head(items):
            return head_grads(items[0], items[1], items[2], items[3], documents)
        query_grads, key_gradient_rows, value_gradient_rows = lax.map(per_head, (query_heads, key_head_states, value_head_states, grad_heads))
        query_grad = query_grads.transpose(1, 0, 2).reshape(TRAJECTORY_TOKENS, QUERY_HEADS * HEAD_SIZE)
        key_gradient_sum = lax.optimization_barrier(jnp.sum(key_gradient_rows.reshape(KEY_VALUE_HEADS, query_group_size, TRAJECTORY_TOKENS, HEAD_SIZE), axis=1)).transpose(1, 0, 2).reshape(TRAJECTORY_TOKENS, KEY_VALUE_HEADS * HEAD_SIZE)
        value_gradient_sum = lax.optimization_barrier(jnp.sum(value_gradient_rows.reshape(KEY_VALUE_HEADS, query_group_size, TRAJECTORY_TOKENS, HEAD_SIZE), axis=1)).transpose(1, 0, 2).reshape(TRAJECTORY_TOKENS, KEY_VALUE_HEADS * HEAD_SIZE)
        pair_grad = jnp.concatenate([key_gradient_sum, value_gradient_sum], axis=1).astype(jnp.bfloat16)
        running = running + jnp.dot(hidden_row.T, pair_grad, preferred_element_type=jnp.float32)
        return (running, query_grad)
    starting_gradient = jnp.zeros((MODEL_WIDTH, 2 * KEY_VALUE_HEADS * HEAD_SIZE), jnp.float32)
    weight_grad, query_grad = lax.scan(trajectory, starting_gradient, (hidden, query_states, saved_key_states, saved_value_states, out_grad, seg_lengths))
    row_norm = jnp.sqrt(lax.optimization_barrier(jnp.mean(weight_grad * weight_grad, axis=1, keepdims=True)) + 1e-06)
    updated = (weights * (1.0 - learn_rate * decay_rate) - learn_rate * weight_grad / row_norm).astype(jnp.bfloat16)
    return (query_grad, updated)
```

```python
import functools
import math

import jax
import jax.numpy as jnp
from jax import lax
from jax.experimental import pallas as pl
from jax.experimental.pallas import tpu as pltpu
from jax.sharding import PartitionSpec as P

KEY_VALUE_HEADS = 2
HEAD_SIZE = 128
learn_rate = 0.5
decay_rate = 0.1
F32 = jnp.float32
BF16 = jnp.bfloat16
MESH = pl.DeviceIdType.MESH


def contract(a, b, dim_a, dim_b):
    return lax.dot_general(a, b, (((dim_a,), (dim_b,)), ((), ())), preferred_element_type=F32)


def kernel(
    plan,
    seg_ref, hidden_ref, query_ref, key_ref, value_ref, grad_ref, weights_ref,
    query_out, updated_ref,
    q_vm, g_vm, dq_vm, k_buf, v_buf, kt_buf, bias_buf, dk_acc, dv_acc,
    part_out, part_in, hid_buf, hidt_buf, pair_buf, wg_buf, wg_half, rs_in, w_vm,
    local_sem, out_sem, kv_out, kv_in, hid_out, hid_in, part_send, part_recv,
    pair_out, pair_recv, fwd_out, fwd_recv, rs_send, rs_recv, up_out, up_recv, upf_out, upf_recv,
):
    S, G, NZ, T, R, W, strips, ndoc = (plan[n] for n in ("S", "G", "NZ", "T", "R", "W", "strips", "ndoc"))
    C = S // 2
    D = HEAD_SIZE
    heads = query_ref.shape[2] // D
    per_group = heads // KEY_VALUE_HEADS
    scale = D ** -0.5
    d = lax.axis_index("dp")
    s = lax.axis_index("seq")
    z, y = d // G, d % G
    chip, core = s // 2, s % 2
    sibling = (d, chip * 2 + 1 - core)

    def member(dy, dc, pc):
        to_core = core if pc == 0 else 1 - core
        return (z * G + (y + dy) % G, ((chip + dc) % C) * 2 + to_core)

    offsets = [(dy, dc, pc) for dy in range(G) for dc in range(C) for pc in range(2)]
    slot = {o: i for i, o in enumerate(offsets)}
    spread = [o for o in offsets if o[2] == 0]

    loads = [
        pltpu.make_async_copy(key_ref.at[0], k_buf.at[pl.ds(W * T, T)], local_sem.at[0]),
        pltpu.make_async_copy(value_ref.at[0], v_buf.at[pl.ds(W * T, T)], local_sem.at[1]),
        pltpu.make_async_copy(query_ref.at[0], q_vm, local_sem.at[2]),
        pltpu.make_async_copy(grad_ref.at[0], g_vm, local_sem.at[3]),
        pltpu.make_async_copy(weights_ref, w_vm, local_sem.at[4]),
    ]
    for copy in loads:
        copy.start()

    for back in range(1, W + 1):
        @pl.when(s < back)
        def _(back=back):
            k_buf[pl.ds((W - back) * T, T), :] = jnp.zeros((T, k_buf.shape[1]), BF16)
            v_buf[pl.ds((W - back) * T, T), :] = jnp.zeros((T, v_buf.shape[1]), BF16)

    barrier = pltpu.get_barrier_semaphore()
    peers = [member(*o) for o in offsets[1:]]
    peers += [(((z + dz) % NZ) * G + y, s) for dz in range(1, NZ)]
    for peer in peers:
        pl.semaphore_signal(barrier, inc=1, device_id=peer, device_id_type=MESH)
    pl.semaphore_wait(barrier, len(peers))

    def remote(src, dst, send, recv, peer):
        return pltpu.make_async_remote_copy(
            src_ref=src, dst_ref=dst, send_sem=send, recv_sem=recv,
            device_id=peer, device_id_type=MESH,
        )

    def kv_copies(back):
        to = (d, lax.rem(s + back, S))
        rows = pl.ds((W - back) * T, T)
        return [
            remote(key_ref.at[0], k_buf.at[rows], kv_out.at[0, back - 1], kv_in.at[0, back - 1], to),
            remote(value_ref.at[0], v_buf.at[rows], kv_out.at[1, back - 1], kv_in.at[1, back - 1], to),
        ]

    for back in range(1, W + 1):
        @pl.when(s + back < S)
        def _(back=back):
            for copy in kv_copies(back):
                copy.start()

    query_at = lax.broadcasted_iota(jnp.int32, (1, T), 1) + s * T
    first = jnp.zeros((1, T), jnp.int32)
    end = jnp.int32(0)
    for i in range(ndoc):
        length = seg_ref[0, i]
        end = end + length
        first = first + jnp.where(query_at >= end, length, 0)
    key_at = lax.broadcasted_iota(jnp.int32, ((W + 1) * T, T), 0) + (s - W) * T
    bias = jnp.where((key_at >= first) & (key_at <= query_at), 0.0, -1e30).astype(F32)
    bias_buf[:, :T] = bias
    bias_buf[:, T:] = bias

    def hid_dst(o, zz=None):
        rows = pl.ds(slot[o] * T, T)
        if zz is None:
            return hid_buf.at[rows]
        return hid_buf.at[rows, pl.ds(zz * R, R)]

    def hid_src(o, zz):
        dy, dc, pc = o
        to_d, to_s = member(*o)
        ty = (y + dy) % G
        if strips:
            column = pl.multiple_of(((zz * G + ty) * S + to_s) * R, 128)
            return hidden_ref.at[0, :, pl.ds(column, R)]
        return hidden_ref.at[ty * S + to_s]

    def hid_copies(o):
        i = slot[o]
        pieces = [(hid_src(o, zz), hid_dst(o, zz)) for zz in range(NZ)] if strips else [
            (hid_src(o, None), hid_dst(o))
        ]
        if i == 0:
            return [pltpu.make_async_copy(a, b, hid_in.at[0]) for a, b in pieces]
        return [remote(a, b, hid_out.at[i], hid_in.at[i], member(*o)) for a, b in pieces]

    def hid_whole(o, sem):
        return pltpu.make_async_copy(hid_dst(o), hid_dst(o), sem)

    for o in offsets:
        for copy in hid_copies(o):
            copy.start()

    for copy in loads:
        copy.wait()
    for back in range(1, W + 1):
        @pl.when(s >= back)
        def _(back=back):
            for copy in kv_copies(back):
                copy.wait_recv()

    def attention(g):
        columns = pl.ds(g * D, D)
        kt_buf[...] = k_buf[:, columns].T
        dk_acc[...] = jnp.zeros_like(dk_acc)
        dv_acc[...] = jnp.zeros_like(dv_acc)

        def pair(i, carry):
            at = pl.multiple_of((g * per_group + 2 * i) * D, 2 * D)
            q2 = q_vm[:, pl.ds(at, 2 * D)]
            q2 = jnp.concatenate([q2[:, :D], q2[:, D:]], axis=0)
            g2 = g_vm[:, pl.ds(at, 2 * D)]
            g2 = jnp.concatenate([g2[:, :D], g2[:, D:]], axis=0)
            scores = contract(k_buf[:, columns], q2, 1, 1)
            scores = scores * (scale * math.log2(math.e)) + bias_buf[...]
            shifted = jnp.exp2(scores - jnp.max(scores, axis=0, keepdims=True))
            attend = shifted * (1.0 / jnp.sum(shifted, axis=0, keepdims=True))
            prob_grad = contract(v_buf[:, columns], g2, 1, 1)
            delta = jnp.sum(attend * prob_grad, axis=0, keepdims=True)
            score_grad = (attend * (prob_grad - delta)).astype(BF16)
            dk_acc[...] += contract(score_grad, q2, 1, 0)
            dv_acc[...] += contract(attend.astype(BF16), g2, 1, 0)
            dq = (contract(kt_buf[...], score_grad, 1, 0) * scale).T.astype(BF16)
            dq_vm[:, pl.ds(at, 2 * D)] = jnp.concatenate([dq[:T], dq[T:]], axis=1)
            return carry

        lax.fori_loop(0, per_group // 2, pair, 0)

    def dq_copy(g):
        columns = pl.ds(g * per_group * D, per_group * D)
        return pltpu.make_async_copy(dq_vm.at[:, columns], query_out.at[0, :, columns], out_sem.at[g])

    def part_copy(g, back):
        to = (d, lax.rem(s - back + S, S))
        return remote(
            part_out.at[g, back - 1], part_in.at[g, back - 1],
            part_send.at[g, back - 1], part_recv.at[g, back - 1], to,
        )

    def send_parts(g):
        dq_copy(g).start()
        for back in range(1, W + 1):
            @pl.when(s >= back)
            def _(back=back):
                rows = pl.ds((W - back) * T, T)
                part_out[g, back - 1, :, :D] = dk_acc[rows, :].astype(BF16)
                part_out[g, back - 1, :, D:] = dv_acc[rows, :].astype(BF16)
                part_copy(g, back).start()

    def pair_copy(g, o):
        i = slot[o]
        return remote(
            pair_buf.at[g, pl.ds(0, T)], pair_buf.at[g, pl.ds(i * T, T)],
            pair_out.at[g, i], pair_recv.at[g, i], member(*o),
        )

    def forward_copy(g, o):
        i = slot[o]
        return remote(
            pair_buf.at[g, pl.ds(i * T, T)], pair_buf.at[g, pl.ds((i + 1) * T, T)],
            fwd_out.at[g, i], fwd_recv.at[g, i], sibling,
        )

    def own_sum(g):
        rows = pl.ds(W * T, T)
        return dk_acc[rows, :], dv_acc[rows, :]

    def send_pairs(g, own):
        dk, dv = own
        for back in range(1, W + 1):
            @pl.when(s + back < S)
            def _(back=back):
                part_copy(g, back).wait_recv()
            here = s + back < S
            got = part_in[g, back - 1]
            dk = dk + jnp.where(here, got[:, :D].astype(F32), 0.0)
            dv = dv + jnp.where(here, got[:, D:].astype(F32), 0.0)
        pair_buf[g, pl.ds(0, T), :D] = (dk * scale).astype(BF16)
        pair_buf[g, pl.ds(0, T), D:] = dv.astype(BF16)
        for o in spread[1:]:
            pair_copy(g, o).start()
        forward_copy(g, spread[0]).start()

    def forward_pairs(g):
        for o in spread[1:]:
            pair_copy(g, o).wait_recv()
            forward_copy(g, o).start()

    def rs_copy(g, dz):
        to = (z + dz) % NZ
        return remote(
            wg_half.at[g, pl.ds(pl.multiple_of(to * R, R), R)], rs_in.at[g, dz - 1],
            rs_send.at[g, dz - 1], rs_recv.at[g, dz - 1], (to * G + y, s),
        )

    def weight_part(g):
        for o in spread:
            forward_copy(g, o).wait_recv()
        total = contract(hidt_buf[...], pair_buf[g], 1, 0)
        wg_buf[g] = total
        wg_half[g] = total.astype(BF16)
        for dz in range(1, NZ):
            rs_copy(g, dz).start()

    for back in range(1, W + 1):
        @pl.when(s + back >= S)
        def _(back=back):
            for g in range(KEY_VALUE_HEADS):
                part_in[g, back - 1] = jnp.zeros(part_in.shape[2:], BF16)

    attention(0)
    send_parts(0)
    own = own_sum(0)
    send_pairs(0, own)
    attention(1)
    send_parts(1)
    forward_pairs(0)
    send_pairs(1, own_sum(1))
    for o in offsets:
        hid_whole(o, hid_in.at[slot[o]]).wait()
        rows = pl.ds(slot[o] * T, T)
        hidt_buf[:, rows] = hid_buf[rows, :].T
    weight_part(0)
    forward_pairs(1)
    weight_part(1)

    mine = pl.ds(pl.multiple_of(z * R, R), R)
    grads = []
    for g in range(KEY_VALUE_HEADS):
        total = wg_buf[g, mine, :]
        for dz in range(1, NZ):
            rs_copy(g, dz).wait_recv()
            total = total + rs_in[g, dz - 1].astype(F32)
        grads.append(total)
    width = weights_ref.shape[1]
    square = sum(jnp.sum(t * t, axis=1, keepdims=True) for t in grads)
    factor = learn_rate / jnp.sqrt(square * (1.0 / width) + 1e-6)
    keep = 1.0 - learn_rate * decay_rate

    def rows_of(owner):
        return pl.ds(pl.multiple_of(owner * R, R), R)

    for g in range(KEY_VALUE_HEADS):
        for kind in range(2):
            columns = pl.ds((kind * KEY_VALUE_HEADS + g) * D, D)
            updated_ref[rows_of(s), columns] = (
                w_vm[:, columns] * keep - grads[g][:, kind * D : (kind + 1) * D] * factor
            ).astype(BF16)

    def up_copy(dc):
        rows = updated_ref.at[rows_of(s)]
        return remote(rows, rows, up_out.at[dc], up_recv.at[dc], (d, ((chip + dc) % C) * 2 + core))

    def up_forward(dc):
        origin = ((chip + C - dc) % C) * 2 + core
        rows = updated_ref.at[rows_of(origin)]
        return remote(rows, rows, upf_out.at[dc], upf_recv.at[dc], sibling)

    for dc in range(1, C):
        up_copy(dc).start()
    up_forward(0).start()
    for dc in range(1, C):
        up_copy(dc).wait_recv()
        up_forward(dc).start()
    for dc in range(C):
        up_forward(dc).wait_recv()

    for dc in range(C):
        if dc:
            up_copy(dc).wait_send()
        up_forward(dc).wait_send()
    for back in range(1, W + 1):
        @pl.when(s + back < S)
        def _(back=back):
            for copy in kv_copies(back):
                copy.wait_send()

        @pl.when(s >= back)
        def _(back=back):
            for g in range(KEY_VALUE_HEADS):
                part_copy(g, back).wait_send()
    for o in offsets[1:]:
        hid_whole(o, hid_out.at[slot[o]]).wait()
    for g in range(KEY_VALUE_HEADS):
        for o in spread:
            if slot[o]:
                pair_copy(g, o).wait_send()
            forward_copy(g, o).wait_send()
        for dz in range(1, NZ):
            rs_copy(g, dz).wait_send()
        dq_copy(g).wait()


def body(hidden, query_states, keys, values, out_grad, seg_lengths, weights):
    S = lax.axis_size("seq")
    dp = lax.axis_size("dp")
    G = 2 if dp % 2 == 0 else 1
    NZ = dp // G
    C = S // 2
    T = hidden.shape[1]
    R, width = weights.shape
    W = S // 2
    D = HEAD_SIZE
    KV = KEY_VALUE_HEADS
    members = G * S
    strips = R % 128 == 0
    if not strips:
        hidden = hidden[0].reshape(T, NZ, G, S, R).transpose(2, 3, 0, 1, 4).reshape(members, T, NZ * R)
    plan = dict(S=S, G=G, NZ=NZ, T=T, R=R, W=W, strips=strips, ndoc=seg_lengths.shape[1])
    window = (W + 1) * T
    model = query_states.shape[2]
    dma = pltpu.SemaphoreType.DMA
    any_spec = pl.BlockSpec(memory_space=pl.ANY)
    scratch = [
        pltpu.VMEM((T, model), BF16),
        pltpu.VMEM((T, model), BF16),
        pltpu.VMEM((T, model), BF16),
        pltpu.VMEM((window, KV * D), BF16),
        pltpu.VMEM((window, KV * D), BF16),
        pltpu.VMEM((D, window), BF16),
        pltpu.VMEM((window, 2 * T), F32),
        pltpu.VMEM((window, D), F32),
        pltpu.VMEM((window, D), F32),
        pltpu.VMEM((KV, W, T, 2 * D), BF16),
        pltpu.VMEM((KV, W, T, 2 * D), BF16),
        pltpu.VMEM((members * T, NZ * R), BF16),
        pltpu.VMEM((NZ * R, members * T), BF16),
        pltpu.VMEM((KV, members * T, 2 * D), BF16),
        pltpu.VMEM((KV, NZ * R, 2 * D), F32),
        pltpu.VMEM((KV, NZ * R, 2 * D), BF16),
        pltpu.VMEM((KV, max(NZ - 1, 1), R, 2 * D), BF16),
        pltpu.VMEM((R, width), F32),
        dma((5,)), dma((KV,)), dma((2, W)), dma((2, W)), dma((members,)), dma((members,)),
        dma((KV, W)), dma((KV, W)), dma((KV, members)), dma((KV, members)),
        dma((KV, members)), dma((KV, members)),
        dma((KV, max(NZ - 1, 1))), dma((KV, max(NZ - 1, 1))),
        dma((C,)), dma((C,)), dma((C,)), dma((C,)),
    ]
    return pl.pallas_call(
        functools.partial(kernel, plan),
        out_shape=(
            jax.ShapeDtypeStruct(query_states.shape, BF16),
            jax.ShapeDtypeStruct((S * R, width), BF16),
        ),
        in_specs=[pl.BlockSpec(memory_space=pltpu.SMEM)] + [any_spec] * 6,
        out_specs=(any_spec, pl.BlockSpec(memory_space=pltpu.VMEM)),
        scratch_shapes=scratch,
        compiler_params=pltpu.CompilerParams(
            collective_id=0, has_side_effects=True, vmem_limit_bytes=56 * 1024 * 1024
        ),
    )(seg_lengths, hidden, query_states, keys, values, out_grad, weights)


def solution(mesh):
    placed = (
        P("dp", "seq", None),
        P("dp", "seq", None),
        P("dp", "seq", None),
        P("dp", "seq", None),
        P("dp", "seq", None),
        P("dp", None),
        P(("dp", "seq"), None),
    )
    return jax.shard_map(
        body,
        mesh=mesh,
        in_specs=placed,
        out_specs=(P("dp", "seq", None), P("dp", None)),
        check_vma=False,
    )
```

```python
import functools
import math

import jax
import jax.numpy as jnp
from jax import lax
from jax.experimental import pallas as pl
from jax.experimental.pallas import tpu as pltpu
from jax.sharding import PartitionSpec as P

KEY_VALUE_HEADS = 2
HEAD_SIZE = 128
learn_rate = 0.5
decay_rate = 0.1
F32 = jnp.float32
BF16 = jnp.bfloat16
MESH = pl.DeviceIdType.MESH


def contract(a, b, dim_a, dim_b):
    return lax.dot_general(a, b, (((dim_a,), (dim_b,)), ((), ())), preferred_element_type=F32)


def kernel(
    plan,
    seg_ref, hidden_ref, query_ref, key_ref, value_ref, grad_ref, weights_ref,
    query_out, updated_ref,
    q_vm, g_vm, dq_vm, k_buf, v_buf, kt_buf, bias_buf, dk_acc, dv_acc,
    part_out, part_in, hid_buf, hidt_buf, pair_buf, wg_buf, wg_half, rs_in, w_vm,
    local_sem, out_sem, kv_out, kv_in, hid_out, hid_in, part_send, part_recv,
    pair_out, pair_recv, fwd_out, fwd_recv, rs_send, rs_recv, up_out, up_recv, upf_out, upf_recv,
):
    S, G, NZ, T, R, W, H, strips, ndoc = (
        plan[n] for n in ("S", "G", "NZ", "T", "R", "W", "H", "strips", "ndoc")
    )
    Rh = R // H
    C = S // 2
    D = HEAD_SIZE
    heads = query_ref.shape[2] // D
    per_group = heads // KEY_VALUE_HEADS
    scale = D ** -0.5
    d = lax.axis_index("dp")
    s = lax.axis_index("seq")
    z, y = d // G, d % G
    chip, core = s // 2, s % 2
    sibling = (d, chip * 2 + 1 - core)

    def member(dy, dc, pc):
        to_core = core if pc == 0 else 1 - core
        return (z * G + (y + dy) % G, ((chip + dc) % C) * 2 + to_core)

    offsets = [(dy, dc, pc) for dy in range(G) for dc in range(C) for pc in range(2)]
    slot = {o: i for i, o in enumerate(offsets)}
    spread = [o for o in offsets if o[2] == 0]

    loads = [
        pltpu.make_async_copy(key_ref.at[0], k_buf.at[pl.ds(W * T, T)], local_sem.at[0]),
        pltpu.make_async_copy(value_ref.at[0], v_buf.at[pl.ds(W * T, T)], local_sem.at[1]),
        pltpu.make_async_copy(query_ref.at[0], q_vm, local_sem.at[2]),
        pltpu.make_async_copy(grad_ref.at[0], g_vm, local_sem.at[3]),
        pltpu.make_async_copy(weights_ref, w_vm, local_sem.at[4]),
    ]
    for copy in loads:
        copy.start()

    for back in range(1, W + 1):
        @pl.when(s < back)
        def _(back=back):
            k_buf[pl.ds((W - back) * T, T), :] = jnp.zeros((T, k_buf.shape[1]), BF16)
            v_buf[pl.ds((W - back) * T, T), :] = jnp.zeros((T, v_buf.shape[1]), BF16)

    barrier = pltpu.get_barrier_semaphore()
    peers = [member(*o) for o in offsets[1:]]
    peers += [(((z + dz) % NZ) * G + y, s) for dz in range(1, NZ)]
    for peer in peers:
        pl.semaphore_signal(barrier, inc=1, device_id=peer, device_id_type=MESH)
    pl.semaphore_wait(barrier, len(peers))

    def remote(src, dst, send, recv, peer):
        return pltpu.make_async_remote_copy(
            src_ref=src, dst_ref=dst, send_sem=send, recv_sem=recv,
            device_id=peer, device_id_type=MESH,
        )

    def kv_copies(g, back):
        to = (d, lax.rem(s + back, S))
        rows = pl.ds((W - back) * T, T)
        cols = pl.ds(g * D, D)
        return [
            remote(
                src.at[0, :, cols], dst.at[rows, cols],
                kv_out.at[i, g, back - 1], kv_in.at[i, g, back - 1], to,
            )
            for i, (src, dst) in enumerate(((key_ref, k_buf), (value_ref, v_buf)))
        ]

    for g in range(KEY_VALUE_HEADS):
        for back in range(W, 0, -1):
            @pl.when(s + back < S)
            def _(g=g, back=back):
                for copy in kv_copies(g, back):
                    copy.start()

    query_at = lax.broadcasted_iota(jnp.int32, (1, T), 1) + s * T
    first = jnp.zeros((1, T), jnp.int32)
    end = jnp.int32(0)
    for i in range(ndoc):
        length = seg_ref[0, i]
        end = end + length
        first = first + jnp.where(query_at >= end, length, 0)
    key_at = lax.broadcasted_iota(jnp.int32, ((W + 1) * T, T), 0) + (s - W) * T
    bias = jnp.where((key_at >= first) & (key_at <= query_at), 0.0, -1e30).astype(F32)
    bias_buf[:, :T] = bias
    bias_buf[:, T:] = bias

    def hid_dst(o, zz=None):
        rows = pl.ds(slot[o] * T, T)
        if zz is None:
            return hid_buf.at[rows]
        return hid_buf.at[rows, pl.ds(zz * R, R)]

    def hid_src(o, zz):
        dy, dc, pc = o
        to_d, to_s = member(*o)
        ty = (y + dy) % G
        if strips:
            column = pl.multiple_of(((zz * G + ty) * S + to_s) * R, 128)
            return hidden_ref.at[0, :, pl.ds(column, R)]
        return hidden_ref.at[ty * S + to_s]

    def hid_copies(o):
        i = slot[o]
        pieces = [(hid_src(o, zz), hid_dst(o, zz)) for zz in range(NZ)] if strips else [
            (hid_src(o, None), hid_dst(o))
        ]
        if i == 0:
            return [pltpu.make_async_copy(a, b, hid_in.at[0]) for a, b in pieces]
        return [remote(a, b, hid_out.at[i], hid_in.at[i], member(*o)) for a, b in pieces]

    def hid_whole(o, sem):
        return pltpu.make_async_copy(hid_dst(o), hid_dst(o), sem)

    for o in offsets:
        for copy in hid_copies(o):
            copy.start()

    for copy in loads:
        copy.wait()

    def receive_keys(g):
        for back in range(1, W + 1):
            @pl.when(s >= back)
            def _(back=back):
                for copy in kv_copies(g, back):
                    copy.wait_recv()
        kt_buf[...] = k_buf[:, pl.ds(g * D, D)].T
        dk_acc[g] = jnp.zeros(dk_acc.shape[1:], F32)
        dv_acc[g] = jnp.zeros(dv_acc.shape[1:], F32)

    def attention(g, begin, stop):
        columns = pl.ds(g * D, D)

        def pair(i, carry):
            at = pl.multiple_of((g * per_group + 2 * i) * D, 2 * D)
            q2 = q_vm[:, pl.ds(at, 2 * D)]
            q2 = jnp.concatenate([q2[:, :D], q2[:, D:]], axis=0)
            g2 = g_vm[:, pl.ds(at, 2 * D)]
            g2 = jnp.concatenate([g2[:, :D], g2[:, D:]], axis=0)
            scores = contract(k_buf[:, columns], q2, 1, 1)
            scores = scores * (scale * math.log2(math.e)) + bias_buf[...]
            shifted = jnp.exp2(scores - jnp.max(scores, axis=0, keepdims=True))
            attend = shifted * (1.0 / jnp.sum(shifted, axis=0, keepdims=True))
            prob_grad = contract(v_buf[:, columns], g2, 1, 1)
            delta = jnp.sum(attend * prob_grad, axis=0, keepdims=True)
            score_grad = (attend * (prob_grad - delta)).astype(BF16)
            dk_acc[g] += contract(score_grad, q2, 1, 0)
            dv_acc[g] += contract(attend.astype(BF16), g2, 1, 0)
            dq = (contract(kt_buf[...], score_grad, 1, 0) * scale).T.astype(BF16)
            dq_vm[:, pl.ds(at, 2 * D)] = jnp.concatenate([dq[:T], dq[T:]], axis=1)
            return carry

        lax.fori_loop(begin, stop, pair, 0)

    def dq_copy(g):
        columns = pl.ds(g * per_group * D, per_group * D)
        return pltpu.make_async_copy(dq_vm.at[:, columns], query_out.at[0, :, columns], out_sem.at[g])

    def part_copy(g, back):
        to = (d, lax.rem(s - back + S, S))
        return remote(
            part_out.at[g, back - 1], part_in.at[g, back - 1],
            part_send.at[g, back - 1], part_recv.at[g, back - 1], to,
        )

    def send_parts(g):
        dq_copy(g).start()
        for back in range(1, W + 1):
            @pl.when(s >= back)
            def _(back=back):
                rows = pl.ds((W - back) * T, T)
                part_out[g, back - 1, :, :D] = dk_acc[g, rows, :].astype(BF16)
                part_out[g, back - 1, :, D:] = dv_acc[g, rows, :].astype(BF16)
                part_copy(g, back).start()

    def pair_copy(g, o):
        i = slot[o]
        return remote(
            pair_buf.at[g, pl.ds(0, T)], pair_buf.at[g, pl.ds(i * T, T)],
            pair_out.at[g, i], pair_recv.at[g, i], member(*o),
        )

    def forward_copy(g, o):
        i = slot[o]
        return remote(
            pair_buf.at[g, pl.ds(i * T, T)], pair_buf.at[g, pl.ds((i + 1) * T, T)],
            fwd_out.at[g, i], fwd_recv.at[g, i], sibling,
        )

    def own_sum(g):
        rows = pl.ds(W * T, T)
        return dk_acc[g, rows, :], dv_acc[g, rows, :]

    def send_pairs(g, own):
        dk, dv = own
        for back in range(1, W + 1):
            @pl.when(s + back < S)
            def _(back=back):
                part_copy(g, back).wait_recv()
            here = s + back < S
            got = part_in[g, back - 1]
            dk = dk + jnp.where(here, got[:, :D].astype(F32), 0.0)
            dv = dv + jnp.where(here, got[:, D:].astype(F32), 0.0)
        pair_buf[g, pl.ds(0, T), :D] = (dk * scale).astype(BF16)
        pair_buf[g, pl.ds(0, T), D:] = dv.astype(BF16)
        for o in spread[1:]:
            pair_copy(g, o).start()
        forward_copy(g, spread[0]).start()

    def forward_pairs(g):
        for o in spread[1:]:
            pair_copy(g, o).wait_recv()
            forward_copy(g, o).start()

    def rs_copy(g, h, dz):
        to = (z + dz) % NZ
        rows = pl.ds(pl.multiple_of(to * R + h * Rh, Rh), Rh)
        return remote(
            wg_half.at[g, rows], rs_in.at[g, dz - 1, pl.ds(h * Rh, Rh)],
            rs_send.at[g, h, dz - 1], rs_recv.at[g, h, dz - 1], (to * G + y, s),
        )

    def weight_part(g):
        for o in spread:
            forward_copy(g, o).wait_recv()
        total = contract(hidt_buf[...], pair_buf[g], 1, 0)
        wg_buf[g] = total
        wg_half[g] = total.astype(BF16)
        for h in range(H):
            for dz in range(1, NZ):
                rs_copy(g, h, dz).start()

    for back in range(1, W + 1):
        @pl.when(s + back >= S)
        def _(back=back):
            for g in range(KEY_VALUE_HEADS):
                part_in[g, back - 1] = jnp.zeros(part_in.shape[2:], BF16)

    pairs = per_group // 2
    middle = pairs * 5 // 8
    receive_keys(0)
    attention(0, 0, pairs)
    send_parts(0)
    receive_keys(1)
    attention(1, 0, middle)
    send_pairs(0, own_sum(0))
    attention(1, middle, pairs)
    send_parts(1)
    for o in offsets:
        hid_whole(o, hid_in.at[slot[o]]).wait()
        rows = pl.ds(slot[o] * T, T)
        hidt_buf[:, rows] = hid_buf[rows, :].T
    send_pairs(1, own_sum(1))
    forward_pairs(0)
    weight_part(0)
    forward_pairs(1)
    weight_part(1)

    width = weights_ref.shape[1]
    keep = 1.0 - learn_rate * decay_rate

    def rows_of(owner, h):
        return pl.ds(pl.multiple_of(owner * R + h * Rh, Rh), Rh)

    def up_copy(h, dc):
        rows = updated_ref.at[rows_of(s, h)]
        to = (d, ((chip + dc) % C) * 2 + core)
        return remote(rows, rows, up_out.at[h, dc], up_recv.at[h, dc], to)

    def up_forward(h, dc):
        origin = ((chip + C - dc) % C) * 2 + core
        rows = updated_ref.at[rows_of(origin, h)]
        return remote(rows, rows, upf_out.at[h, dc], upf_recv.at[h, dc], sibling)

    for h in range(H):
        grads = []
        for g in range(KEY_VALUE_HEADS):
            total = wg_buf[g, rows_of(z, h), :]
            for dz in range(1, NZ):
                rs_copy(g, h, dz).wait_recv()
                total = total + rs_in[g, dz - 1, pl.ds(h * Rh, Rh)].astype(F32)
            grads.append(total)
        square = sum(jnp.sum(t * t, axis=1, keepdims=True) for t in grads)
        factor = learn_rate / jnp.sqrt(square * (1.0 / width) + 1e-6)
        for g in range(KEY_VALUE_HEADS):
            for kind in range(2):
                columns = pl.ds((kind * KEY_VALUE_HEADS + g) * D, D)
                updated_ref[rows_of(s, h), columns] = (
                    w_vm[pl.ds(h * Rh, Rh), columns] * keep
                    - grads[g][:, kind * D : (kind + 1) * D] * factor
                ).astype(BF16)
        for dc in range(1, C):
            up_copy(h, dc).start()
        up_forward(h, 0).start()
    for h in range(H):
        for dc in range(1, C):
            up_copy(h, dc).wait_recv()
            up_forward(h, dc).start()
    for h in range(H):
        for dc in range(C):
            up_forward(h, dc).wait_recv()

    for h in range(H):
        for dc in range(C):
            if dc:
                up_copy(h, dc).wait_send()
            up_forward(h, dc).wait_send()
    for back in range(1, W + 1):
        @pl.when(s + back < S)
        def _(back=back):
            for g in range(KEY_VALUE_HEADS):
                for copy in kv_copies(g, back):
                    copy.wait_send()

        @pl.when(s >= back)
        def _(back=back):
            for g in range(KEY_VALUE_HEADS):
                part_copy(g, back).wait_send()
    for o in offsets[1:]:
        hid_whole(o, hid_out.at[slot[o]]).wait()
    for g in range(KEY_VALUE_HEADS):
        for o in spread:
            if slot[o]:
                pair_copy(g, o).wait_send()
            forward_copy(g, o).wait_send()
        for h in range(H):
            for dz in range(1, NZ):
                rs_copy(g, h, dz).wait_send()
        dq_copy(g).wait()


def body(hidden, query_states, keys, values, out_grad, seg_lengths, weights):
    S = lax.axis_size("seq")
    dp = lax.axis_size("dp")
    G = 2 if dp % 2 == 0 else 1
    NZ = dp // G
    C = S // 2
    T = hidden.shape[1]
    R, width = weights.shape
    W = S // 2
    D = HEAD_SIZE
    KV = KEY_VALUE_HEADS
    members = G * S
    strips = R % 128 == 0
    if not strips:
        hidden = hidden[0].reshape(T, NZ, G, S, R).transpose(2, 3, 0, 1, 4).reshape(members, T, NZ * R)
    H = 2 if R % 32 == 0 else 1
    plan = dict(S=S, G=G, NZ=NZ, T=T, R=R, W=W, H=H, strips=strips, ndoc=seg_lengths.shape[1])
    window = (W + 1) * T
    model = query_states.shape[2]
    dma = pltpu.SemaphoreType.DMA
    any_spec = pl.BlockSpec(memory_space=pl.ANY)
    scratch = [
        pltpu.VMEM((T, model), BF16),
        pltpu.VMEM((T, model), BF16),
        pltpu.VMEM((T, model), BF16),
        pltpu.VMEM((window, KV * D), BF16),
        pltpu.VMEM((window, KV * D), BF16),
        pltpu.VMEM((D, window), BF16),
        pltpu.VMEM((window, 2 * T), F32),
        pltpu.VMEM((KV, window, D), F32),
        pltpu.VMEM((KV, window, D), F32),
        pltpu.VMEM((KV, W, T, 2 * D), BF16),
        pltpu.VMEM((KV, W, T, 2 * D), BF16),
        pltpu.VMEM((members * T, NZ * R), BF16),
        pltpu.VMEM((NZ * R, members * T), BF16),
        pltpu.VMEM((KV, members * T, 2 * D), BF16),
        pltpu.VMEM((KV, NZ * R, 2 * D), F32),
        pltpu.VMEM((KV, NZ * R, 2 * D), BF16),
        pltpu.VMEM((KV, max(NZ - 1, 1), R, 2 * D), BF16),
        pltpu.VMEM((R, width), F32),
        dma((5,)), dma((KV,)), dma((2, KV, W)), dma((2, KV, W)), dma((members,)), dma((members,)),
        dma((KV, W)), dma((KV, W)), dma((KV, members)), dma((KV, members)),
        dma((KV, members)), dma((KV, members)),
        dma((KV, H, max(NZ - 1, 1))), dma((KV, H, max(NZ - 1, 1))),
        dma((H, C)), dma((H, C)), dma((H, C)), dma((H, C)),
    ]
    return pl.pallas_call(
        functools.partial(kernel, plan),
        out_shape=(
            jax.ShapeDtypeStruct(query_states.shape, BF16),
            jax.ShapeDtypeStruct((S * R, width), BF16),
        ),
        in_specs=[pl.BlockSpec(memory_space=pltpu.SMEM)] + [any_spec] * 6,
        out_specs=(any_spec, pl.BlockSpec(memory_space=pltpu.VMEM)),
        scratch_shapes=scratch,
        compiler_params=pltpu.CompilerParams(
            collective_id=0, has_side_effects=True, vmem_limit_bytes=56 * 1024 * 1024
        ),
    )(seg_lengths, hidden, query_states, keys, values, out_grad, weights)


def solution(mesh):
    placed = (
        P("dp", "seq", None),
        P("dp", "seq", None),
        P("dp", "seq", None),
        P("dp", "seq", None),
        P("dp", "seq", None),
        P("dp", None),
        P(("dp", "seq"), None),
    )
    return jax.shard_map(
        body,
        mesh=mesh,
        in_specs=placed,
        out_specs=(P("dp", "seq", None), P("dp", None)),
        check_vma=False,
    )
```

```python
import functools
import math

import jax
import jax.numpy as jnp
from jax import lax
from jax.experimental import pallas as pl
from jax.experimental.pallas import tpu as pltpu
from jax.sharding import PartitionSpec as P

KEY_VALUE_HEADS = 2
HEAD_SIZE = 128
learn_rate = 0.5
decay_rate = 0.1
F32 = jnp.float32
BF16 = jnp.bfloat16
MESH = pl.DeviceIdType.MESH


def contract(a, b, dim_a, dim_b):
    return lax.dot_general(a, b, (((dim_a,), (dim_b,)), ((), ())), preferred_element_type=F32)


def kernel(
    plan,
    seg_ref, hidden_ref, query_ref, key_ref, value_ref, grad_ref, weights_ref,
    query_out, updated_ref,
    q_vm, g_vm, dq_vm, k_buf, v_buf, kt_buf, bias_buf, dk_acc, dv_acc,
    part_out, part_in, hid_buf, hidt_buf, pair_buf, wg_buf, wg_half, rs_in, w_vm,
    local_sem, out_sem, kv_out, kv_in, hid_out, hid_in, part_send, part_recv,
    pair_out, pair_recv, fwd_out, fwd_recv, rs_send, rs_recv, up_out, up_recv, upf_out, upf_recv,
):
    S, G, NZ, T, R, W, H, strips, ndoc = (
        plan[n] for n in ("S", "G", "NZ", "T", "R", "W", "H", "strips", "ndoc")
    )
    Rh = R // H
    C = S // 2
    D = HEAD_SIZE
    heads = query_ref.shape[2] // D
    per_group = heads // KEY_VALUE_HEADS
    scale = D ** -0.5
    d = lax.axis_index("dp")
    s = lax.axis_index("seq")
    z, y = d // G, d % G
    chip, core = s // 2, s % 2
    sibling = (d, chip * 2 + 1 - core)

    def member(dy, dc, pc):
        to_core = core if pc == 0 else 1 - core
        return (z * G + (y + dy) % G, ((chip + dc) % C) * 2 + to_core)

    offsets = [(dy, dc, pc) for dy in range(G) for dc in range(C) for pc in range(2)]
    slot = {o: i for i, o in enumerate(offsets)}
    spread = [o for o in offsets if o[2] == 0]

    loads = [
        pltpu.make_async_copy(key_ref.at[0], k_buf.at[pl.ds(W * T, T)], local_sem.at[0]),
        pltpu.make_async_copy(value_ref.at[0], v_buf.at[pl.ds(W * T, T)], local_sem.at[1]),
        pltpu.make_async_copy(query_ref.at[0], q_vm, local_sem.at[2]),
        pltpu.make_async_copy(grad_ref.at[0], g_vm, local_sem.at[3]),
        pltpu.make_async_copy(weights_ref, w_vm, local_sem.at[4]),
    ]
    for copy in loads:
        copy.start()

    for back in range(1, W + 1):
        @pl.when(s < back)
        def _(back=back):
            k_buf[pl.ds((W - back) * T, T), :] = jnp.zeros((T, k_buf.shape[1]), BF16)
            v_buf[pl.ds((W - back) * T, T), :] = jnp.zeros((T, v_buf.shape[1]), BF16)

    barrier = pltpu.get_barrier_semaphore()
    peers = [member(*o) for o in offsets[1:]]
    peers += [(((z + dz) % NZ) * G + y, s) for dz in range(1, NZ)]
    for peer in peers:
        pl.semaphore_signal(barrier, inc=1, device_id=peer, device_id_type=MESH)
    pl.semaphore_wait(barrier, len(peers))

    def remote(src, dst, send, recv, peer):
        return pltpu.make_async_remote_copy(
            src_ref=src, dst_ref=dst, send_sem=send, recv_sem=recv,
            device_id=peer, device_id_type=MESH,
        )

    def kv_copies(g, back):
        to = (d, lax.rem(s + back, S))
        rows = pl.ds((W - back) * T, T)
        cols = pl.ds(g * D, D)
        return [
            remote(
                src.at[0, :, cols], dst.at[rows, cols],
                kv_out.at[i, g, back - 1], kv_in.at[i, g, back - 1], to,
            )
            for i, (src, dst) in enumerate(((key_ref, k_buf), (value_ref, v_buf)))
        ]

    for g in range(KEY_VALUE_HEADS):
        for back in range(W, 0, -1):
            @pl.when(s + back < S)
            def _(g=g, back=back):
                for copy in kv_copies(g, back):
                    copy.start()

    query_at = lax.broadcasted_iota(jnp.int32, (1, T), 1) + s * T
    first = jnp.zeros((1, T), jnp.int32)
    end = jnp.int32(0)
    for i in range(ndoc):
        length = seg_ref[0, i]
        end = end + length
        first = first + jnp.where(query_at >= end, length, 0)
    key_at = lax.broadcasted_iota(jnp.int32, ((W + 1) * T, T), 0) + (s - W) * T
    bias = jnp.where((key_at >= first) & (key_at <= query_at), 0.0, -1e30).astype(F32)
    bias_buf[:, :T] = bias
    bias_buf[:, T:] = bias

    def hid_dst(o, zz=None):
        rows = pl.ds(slot[o] * T, T)
        if zz is None:
            return hid_buf.at[rows]
        return hid_buf.at[rows, pl.ds(zz * R, R)]

    def hid_src(o, zz):
        dy, dc, pc = o
        to_d, to_s = member(*o)
        ty = (y + dy) % G
        if strips:
            column = pl.multiple_of(((zz * G + ty) * S + to_s) * R, 128)
            return hidden_ref.at[0, :, pl.ds(column, R)]
        return hidden_ref.at[ty * S + to_s]

    def hid_copies(o):
        i = slot[o]
        pieces = [(hid_src(o, zz), hid_dst(o, zz)) for zz in range(NZ)] if strips else [
            (hid_src(o, None), hid_dst(o))
        ]
        if i == 0:
            return [pltpu.make_async_copy(a, b, hid_in.at[0]) for a, b in pieces]
        return [remote(a, b, hid_out.at[i], hid_in.at[i], member(*o)) for a, b in pieces]

    def hid_whole(o, sem):
        return pltpu.make_async_copy(hid_dst(o), hid_dst(o), sem)

    for o in offsets:
        for copy in hid_copies(o):
            copy.start()

    for copy in loads:
        copy.wait()

    def receive_keys(g):
        for back in range(1, W + 1):
            @pl.when(s >= back)
            def _(back=back):
                for copy in kv_copies(g, back):
                    copy.wait_recv()
        kt_buf[...] = k_buf[:, pl.ds(g * D, D)].T
        dk_acc[g] = jnp.zeros(dk_acc.shape[1:], F32)
        dv_acc[g] = jnp.zeros(dv_acc.shape[1:], F32)

    def attention(g, begin, stop):
        columns = pl.ds(g * D, D)

        def pair(i, carry):
            at = pl.multiple_of((g * per_group + 2 * i) * D, 2 * D)
            q2 = q_vm[:, pl.ds(at, 2 * D)]
            q2 = jnp.concatenate([q2[:, :D], q2[:, D:]], axis=0)
            g2 = g_vm[:, pl.ds(at, 2 * D)]
            g2 = jnp.concatenate([g2[:, :D], g2[:, D:]], axis=0)
            scores = contract(k_buf[:, columns], q2, 1, 1)
            scores = scores * (scale * math.log2(math.e)) + bias_buf[...]
            shifted = jnp.exp2(scores - jnp.max(scores, axis=0, keepdims=True))
            attend = shifted * (1.0 / jnp.sum(shifted, axis=0, keepdims=True))
            prob_grad = contract(v_buf[:, columns], g2, 1, 1)
            delta = jnp.sum(attend * prob_grad, axis=0, keepdims=True)
            score_grad = (attend * (prob_grad - delta)).astype(BF16)
            dk_acc[g] += contract(score_grad, q2, 1, 0)
            dv_acc[g] += contract(attend.astype(BF16), g2, 1, 0)
            dq = (contract(kt_buf[...], score_grad, 1, 0) * scale).T.astype(BF16)
            dq_vm[:, pl.ds(at, 2 * D)] = jnp.concatenate([dq[:T], dq[T:]], axis=1)
            return carry

        lax.fori_loop(begin, stop, pair, 0)

    def dq_copy(g):
        columns = pl.ds(g * per_group * D, per_group * D)
        return pltpu.make_async_copy(dq_vm.at[:, columns], query_out.at[0, :, columns], out_sem.at[g])

    def part_copy(g, back):
        to = (d, lax.rem(s - back + S, S))
        return remote(
            part_out.at[g, back - 1], part_in.at[g, back - 1],
            part_send.at[g, back - 1], part_recv.at[g, back - 1], to,
        )

    def send_parts(g):
        dq_copy(g).start()
        for back in range(1, W + 1):
            @pl.when(s >= back)
            def _(back=back):
                rows = pl.ds((W - back) * T, T)
                part_out[g, back - 1, :, :D] = dk_acc[g, rows, :].astype(BF16)
                part_out[g, back - 1, :, D:] = dv_acc[g, rows, :].astype(BF16)
                part_copy(g, back).start()

    def pair_copy(g, o):
        i = slot[o]
        return remote(
            pair_buf.at[g, pl.ds(0, T)], pair_buf.at[g, pl.ds(i * T, T)],
            pair_out.at[g, i], pair_recv.at[g, i], member(*o),
        )

    def forward_copy(g, o):
        i = slot[o]
        return remote(
            pair_buf.at[g, pl.ds(i * T, T)], pair_buf.at[g, pl.ds((i + 1) * T, T)],
            fwd_out.at[g, i], fwd_recv.at[g, i], sibling,
        )

    def own_sum(g):
        rows = pl.ds(W * T, T)
        return dk_acc[g, rows, :], dv_acc[g, rows, :]

    def send_pairs(g, own):
        dk, dv = own
        for back in range(1, W + 1):
            @pl.when(s + back < S)
            def _(back=back):
                part_copy(g, back).wait_recv()
            here = s + back < S
            got = part_in[g, back - 1]
            dk = dk + jnp.where(here, got[:, :D].astype(F32), 0.0)
            dv = dv + jnp.where(here, got[:, D:].astype(F32), 0.0)
        pair_buf[g, pl.ds(0, T), :D] = (dk * scale).astype(BF16)
        pair_buf[g, pl.ds(0, T), D:] = dv.astype(BF16)
        for o in spread[1:]:
            pair_copy(g, o).start()
        forward_copy(g, spread[0]).start()

    def forward_pairs(g):
        for o in spread[1:]:
            pair_copy(g, o).wait_recv()
            forward_copy(g, o).start()

    def rs_copy(g, h, dz):
        to = (z + dz) % NZ
        rows = pl.ds(pl.multiple_of(to * R + h * Rh, Rh), Rh)
        return remote(
            wg_half.at[g, rows], rs_in.at[g, dz - 1, pl.ds(h * Rh, Rh)],
            rs_send.at[g, h, dz - 1], rs_recv.at[g, h, dz - 1], (to * G + y, s),
        )

    def weight_part(g):
        for o in spread:
            forward_copy(g, o).wait_recv()
        total = contract(hidt_buf[...], pair_buf[g], 1, 0)
        wg_buf[g] = total
        wg_half[g] = total.astype(BF16)
        for h in range(H):
            for dz in range(1, NZ):
                rs_copy(g, h, dz).start()

    for back in range(1, W + 1):
        @pl.when(s + back >= S)
        def _(back=back):
            for g in range(KEY_VALUE_HEADS):
                part_in[g, back - 1] = jnp.zeros(part_in.shape[2:], BF16)

    pairs = per_group // 2
    middle = pairs * 5 // 8
    receive_keys(0)
    attention(0, 0, pairs)
    send_parts(0)
    receive_keys(1)
    attention(1, 0, middle)
    send_pairs(0, own_sum(0))
    attention(1, middle, pairs)
    send_parts(1)
    send_pairs(1, own_sum(1))
    forward_pairs(0)
    for o in offsets:
        hid_whole(o, hid_in.at[slot[o]]).wait()
        rows = pl.ds(slot[o] * T, T)
        hidt_buf[:, rows] = hid_buf[rows, :].T
    weight_part(0)
    forward_pairs(1)
    weight_part(1)

    width = weights_ref.shape[1]
    keep = 1.0 - learn_rate * decay_rate

    def rows_of(owner, h):
        return pl.ds(pl.multiple_of(owner * R + h * Rh, Rh), Rh)

    def up_copy(h, dc):
        rows = updated_ref.at[rows_of(s, h)]
        to = (d, ((chip + dc) % C) * 2 + core)
        return remote(rows, rows, up_out.at[h, dc], up_recv.at[h, dc], to)

    def up_forward(h, dc):
        origin = ((chip + C - dc) % C) * 2 + core
        rows = updated_ref.at[rows_of(origin, h)]
        return remote(rows, rows, upf_out.at[h, dc], upf_recv.at[h, dc], sibling)

    for h in range(H):
        grads = []
        for g in range(KEY_VALUE_HEADS):
            total = wg_buf[g, rows_of(z, h), :]
            for dz in range(1, NZ):
                rs_copy(g, h, dz).wait_recv()
                total = total + rs_in[g, dz - 1, pl.ds(h * Rh, Rh)].astype(F32)
            grads.append(total)
        square = sum(jnp.sum(t * t, axis=1, keepdims=True) for t in grads)
        factor = learn_rate / jnp.sqrt(square * (1.0 / width) + 1e-6)
        for g in range(KEY_VALUE_HEADS):
            for kind in range(2):
                columns = pl.ds((kind * KEY_VALUE_HEADS + g) * D, D)
                updated_ref[rows_of(s, h), columns] = (
                    w_vm[pl.ds(h * Rh, Rh), columns] * keep
                    - grads[g][:, kind * D : (kind + 1) * D] * factor
                ).astype(BF16)
        for dc in range(1, C):
            up_copy(h, dc).start()
        up_forward(h, 0).start()
    for h in range(H):
        for dc in range(1, C):
            up_copy(h, dc).wait_recv()
            up_forward(h, dc).start()
    for h in range(H):
        for dc in range(C):
            up_forward(h, dc).wait_recv()

    for h in range(H):
        for dc in range(C):
            if dc:
                up_copy(h, dc).wait_send()
            up_forward(h, dc).wait_send()
    for back in range(1, W + 1):
        @pl.when(s + back < S)
        def _(back=back):
            for g in range(KEY_VALUE_HEADS):
                for copy in kv_copies(g, back):
                    copy.wait_send()

        @pl.when(s >= back)
        def _(back=back):
            for g in range(KEY_VALUE_HEADS):
                part_copy(g, back).wait_send()
    for o in offsets[1:]:
        hid_whole(o, hid_out.at[slot[o]]).wait()
    for g in range(KEY_VALUE_HEADS):
        for o in spread:
            if slot[o]:
                pair_copy(g, o).wait_send()
            forward_copy(g, o).wait_send()
        for h in range(H):
            for dz in range(1, NZ):
                rs_copy(g, h, dz).wait_send()
        dq_copy(g).wait()


def place(query_in, updated_in, query_out, updated_out, sem):
    rows = query_in.shape[1] // 8
    copies = [
        pltpu.make_async_copy(query_in.at[0, pl.ds(i * rows, rows)], query_out.at[0, pl.ds(i * rows, rows)], sem.at[i])
        for i in range(8)
    ]
    copies.append(pltpu.make_async_copy(updated_in, updated_out, sem.at[8]))
    for copy in copies:
        copy.start()
    for copy in copies:
        copy.wait()


def body(hidden, query_states, keys, values, out_grad, seg_lengths, weights):
    S = lax.axis_size("seq")
    dp = lax.axis_size("dp")
    G = 2 if dp % 2 == 0 else 1
    NZ = dp // G
    C = S // 2
    T = hidden.shape[1]
    R, width = weights.shape
    W = S // 2
    D = HEAD_SIZE
    KV = KEY_VALUE_HEADS
    members = G * S
    strips = R % 128 == 0
    if not strips:
        hidden = hidden[0].reshape(T, NZ, G, S, R).transpose(2, 3, 0, 1, 4).reshape(members, T, NZ * R)
    H = 2 if R % 32 == 0 else 1
    plan = dict(S=S, G=G, NZ=NZ, T=T, R=R, W=W, H=H, strips=strips, ndoc=seg_lengths.shape[1])
    window = (W + 1) * T
    model = query_states.shape[2]
    dma = pltpu.SemaphoreType.DMA
    any_spec = pl.BlockSpec(memory_space=pl.ANY)
    scratch = [
        pltpu.VMEM((T, model), BF16),
        pltpu.VMEM((T, model), BF16),
        pltpu.VMEM((T, model), BF16),
        pltpu.VMEM((window, KV * D), BF16),
        pltpu.VMEM((window, KV * D), BF16),
        pltpu.VMEM((D, window), BF16),
        pltpu.VMEM((window, 2 * T), F32),
        pltpu.VMEM((KV, window, D), F32),
        pltpu.VMEM((KV, window, D), F32),
        pltpu.VMEM((KV, W, T, 2 * D), BF16),
        pltpu.VMEM((KV, W, T, 2 * D), BF16),
        pltpu.VMEM((members * T, NZ * R), BF16),
        pltpu.VMEM((NZ * R, members * T), BF16),
        pltpu.VMEM((KV, members * T, 2 * D), BF16),
        pltpu.VMEM((KV, NZ * R, 2 * D), F32),
        pltpu.VMEM((KV, NZ * R, 2 * D), BF16),
        pltpu.VMEM((KV, max(NZ - 1, 1), R, 2 * D), BF16),
        pltpu.VMEM((R, width), F32),
        dma((5,)), dma((KV,)), dma((2, KV, W)), dma((2, KV, W)), dma((members,)), dma((members,)),
        dma((KV, W)), dma((KV, W)), dma((KV, members)), dma((KV, members)),
        dma((KV, members)), dma((KV, members)),
        dma((KV, H, max(NZ - 1, 1))), dma((KV, H, max(NZ - 1, 1))),
        dma((H, C)), dma((H, C)), dma((H, C)), dma((H, C)),
    ]
    outs = pl.pallas_call(
        functools.partial(kernel, plan),
        out_shape=(
            jax.ShapeDtypeStruct(query_states.shape, BF16),
            jax.ShapeDtypeStruct((S * R, width), BF16),
        ),
        in_specs=[pl.BlockSpec(memory_space=pltpu.SMEM)] + [any_spec] * 6,
        out_specs=(any_spec, pl.BlockSpec(memory_space=pltpu.VMEM)),
        scratch_shapes=scratch,
        compiler_params=pltpu.CompilerParams(
            collective_id=0, has_side_effects=True, vmem_limit_bytes=56 * 1024 * 1024
        ),
    )(seg_lengths, hidden, query_states, keys, values, out_grad, weights)
    return pl.pallas_call(
        place,
        out_shape=tuple(jax.ShapeDtypeStruct(o.shape, o.dtype) for o in outs),
        in_specs=[pl.BlockSpec(memory_space=pltpu.VMEM)] * 2,
        out_specs=(any_spec,) * 2,
        scratch_shapes=[dma((9,))],
    )(*outs)


def solution(mesh):
    placed = (
        P("dp", "seq", None),
        P("dp", "seq", None),
        P("dp", "seq", None),
        P("dp", "seq", None),
        P("dp", "seq", None),
        P("dp", None),
        P(("dp", "seq"), None),
    )
    return jax.shard_map(
        body,
        mesh=mesh,
        in_specs=placed,
        out_specs=(P("dp", "seq", None), P("dp", None)),
        check_vma=False,
    )
```

```python
import functools
import math

import jax
import jax.numpy as jnp
from jax import lax
from jax.experimental import pallas as pl
from jax.experimental.pallas import tpu as pltpu
from jax.sharding import PartitionSpec as P

KEY_VALUE_HEADS = 2
HEAD_SIZE = 128
learn_rate = 0.5
decay_rate = 0.1
F32 = jnp.float32
BF16 = jnp.bfloat16
MESH = pl.DeviceIdType.MESH


def contract(a, b, dim_a, dim_b):
    return lax.dot_general(a, b, (((dim_a,), (dim_b,)), ((), ())), preferred_element_type=F32)


def kernel(
    plan,
    seg_ref, hidden_ref, query_ref, key_ref, value_ref, grad_ref, weights_ref,
    query_out, updated_ref,
    q_vm, g_vm, dq_vm, k_buf, v_buf, kt_buf, bias_buf, dk_acc, dv_acc,
    part_out, part_in, hid_buf, hidt_buf, pair_buf, wg_buf, wg_half, rs_in, w_vm,
    local_sem, out_sem, kv_out, kv_in, hid_out, hid_in, part_send, part_recv,
    pair_out, pair_recv, fwd_out, fwd_recv, rs_send, rs_recv, up_out, up_recv, upf_out, upf_recv,
):
    S, G, NZ, T, R, W, H, strips, ndoc = (
        plan[n] for n in ("S", "G", "NZ", "T", "R", "W", "H", "strips", "ndoc")
    )
    Rh = R // H
    C = S // 2
    D = HEAD_SIZE
    heads = query_ref.shape[2] // D
    per_group = heads // KEY_VALUE_HEADS
    scale = D ** -0.5
    d = lax.axis_index("dp")
    s = lax.axis_index("seq")
    z, y = d // G, d % G
    chip, core = s // 2, s % 2
    sibling = (d, chip * 2 + 1 - core)

    def member(dy, dc, pc):
        to_core = core if pc == 0 else 1 - core
        return (z * G + (y + dy) % G, ((chip + dc) % C) * 2 + to_core)

    offsets = [(dy, dc, pc) for dy in range(G) for dc in range(C) for pc in range(2)]
    slot = {o: i for i, o in enumerate(offsets)}
    spread = [o for o in offsets if o[2] == 0]

    loads = [
        pltpu.make_async_copy(key_ref.at[0], k_buf.at[pl.ds(W * T, T)], local_sem.at[0]),
        pltpu.make_async_copy(value_ref.at[0], v_buf.at[pl.ds(W * T, T)], local_sem.at[1]),
        pltpu.make_async_copy(query_ref.at[0], q_vm, local_sem.at[2]),
        pltpu.make_async_copy(grad_ref.at[0], g_vm, local_sem.at[3]),
        pltpu.make_async_copy(weights_ref, w_vm, local_sem.at[4]),
    ]
    for copy in loads:
        copy.start()

    for back in range(1, W + 1):
        @pl.when(s < back)
        def _(back=back):
            k_buf[pl.ds((W - back) * T, T), :] = jnp.zeros((T, k_buf.shape[1]), BF16)
            v_buf[pl.ds((W - back) * T, T), :] = jnp.zeros((T, v_buf.shape[1]), BF16)

    barrier = pltpu.get_barrier_semaphore()
    peers = [member(*o) for o in offsets[1:]]
    peers += [(((z + dz) % NZ) * G + y, s) for dz in range(1, NZ)]
    for peer in peers:
        pl.semaphore_signal(barrier, inc=1, device_id=peer, device_id_type=MESH)
    pl.semaphore_wait(barrier, len(peers))

    def remote(src, dst, send, recv, peer):
        return pltpu.make_async_remote_copy(
            src_ref=src, dst_ref=dst, send_sem=send, recv_sem=recv,
            device_id=peer, device_id_type=MESH,
        )

    def kv_copies(g, back):
        to = (d, lax.rem(s + back, S))
        rows = pl.ds((W - back) * T, T)
        cols = pl.ds(g * D, D)
        return [
            remote(
                src.at[0, :, cols], dst.at[rows, cols],
                kv_out.at[i, g, back - 1], kv_in.at[i, g, back - 1], to,
            )
            for i, (src, dst) in enumerate(((key_ref, k_buf), (value_ref, v_buf)))
        ]

    for g in range(KEY_VALUE_HEADS):
        for back in range(W, 0, -1):
            @pl.when(s + back < S)
            def _(g=g, back=back):
                for copy in kv_copies(g, back):
                    copy.start()

    query_at = lax.broadcasted_iota(jnp.int32, (1, T), 1) + s * T
    first = jnp.zeros((1, T), jnp.int32)
    end = jnp.int32(0)
    for i in range(ndoc):
        length = seg_ref[0, i]
        end = end + length
        first = first + jnp.where(query_at >= end, length, 0)
    key_at = lax.broadcasted_iota(jnp.int32, ((W + 1) * T, T), 0) + (s - W) * T
    bias = jnp.where((key_at >= first) & (key_at <= query_at), 0.0, -1e30).astype(F32)
    bias_buf[:, :T] = bias
    bias_buf[:, T:] = bias

    def hid_dst(o, zz=None):
        rows = pl.ds(slot[o] * T, T)
        if zz is None:
            return hid_buf.at[rows]
        return hid_buf.at[rows, pl.ds(zz * R, R)]

    def hid_src(o, zz):
        dy, dc, pc = o
        to_d, to_s = member(*o)
        ty = (y + dy) % G
        if strips:
            column = pl.multiple_of(((zz * G + ty) * S + to_s) * R, 128)
            return hidden_ref.at[0, :, pl.ds(column, R)]
        return hidden_ref.at[ty * S + to_s]

    def hid_copies(o):
        i = slot[o]
        pieces = [(hid_src(o, zz), hid_dst(o, zz)) for zz in range(NZ)] if strips else [
            (hid_src(o, None), hid_dst(o))
        ]
        if i == 0:
            return [pltpu.make_async_copy(a, b, hid_in.at[0]) for a, b in pieces]
        return [remote(a, b, hid_out.at[i], hid_in.at[i], member(*o)) for a, b in pieces]

    def hid_whole(o, sem):
        return pltpu.make_async_copy(hid_dst(o), hid_dst(o), sem)

    for o in offsets:
        for copy in hid_copies(o):
            copy.start()

    for copy in loads:
        copy.wait()

    def receive_keys(g):
        for back in range(1, W + 1):
            @pl.when(s >= back)
            def _(back=back):
                for copy in kv_copies(g, back):
                    copy.wait_recv()
        kt_buf[...] = k_buf[:, pl.ds(g * D, D)].T
        dk_acc[g] = jnp.zeros(dk_acc.shape[1:], F32)
        dv_acc[g] = jnp.zeros(dv_acc.shape[1:], F32)

    def attention(g, begin, stop):
        columns = pl.ds(g * D, D)

        def pair(i, carry):
            at = pl.multiple_of((g * per_group + 2 * i) * D, 2 * D)
            q2 = q_vm[:, pl.ds(at, 2 * D)]
            q2 = jnp.concatenate([q2[:, :D], q2[:, D:]], axis=0)
            g2 = g_vm[:, pl.ds(at, 2 * D)]
            g2 = jnp.concatenate([g2[:, :D], g2[:, D:]], axis=0)
            scores = contract(k_buf[:, columns], q2, 1, 1)
            scores = scores * (scale * math.log2(math.e)) + bias_buf[...]
            shifted = jnp.exp2(scores - jnp.max(scores, axis=0, keepdims=True))
            attend = shifted * (1.0 / jnp.sum(shifted, axis=0, keepdims=True))
            prob_grad = contract(v_buf[:, columns], g2, 1, 1)
            delta = jnp.sum(attend * prob_grad, axis=0, keepdims=True)
            score_grad = (attend * (prob_grad - delta)).astype(BF16)
            dk_acc[g] += contract(score_grad, q2, 1, 0)
            dv_acc[g] += contract(attend.astype(BF16), g2, 1, 0)
            dq = (contract(kt_buf[...], score_grad, 1, 0) * scale).T.astype(BF16)
            dq_vm[:, pl.ds(at, 2 * D)] = jnp.concatenate([dq[:T], dq[T:]], axis=1)
            return carry

        lax.fori_loop(begin, stop, pair, 0, unroll=2)

    def dq_copy(g):
        columns = pl.ds(g * per_group * D, per_group * D)
        return pltpu.make_async_copy(dq_vm.at[:, columns], query_out.at[0, :, columns], out_sem.at[g])

    def part_copy(g, back):
        to = (d, lax.rem(s - back + S, S))
        return remote(
            part_out.at[g, back - 1], part_in.at[g, back - 1],
            part_send.at[g, back - 1], part_recv.at[g, back - 1], to,
        )

    def send_parts(g):
        dq_copy(g).start()
        for back in range(1, W + 1):
            @pl.when(s >= back)
            def _(back=back):
                rows = pl.ds((W - back) * T, T)
                part_out[g, back - 1, :, :D] = dk_acc[g, rows, :].astype(BF16)
                part_out[g, back - 1, :, D:] = dv_acc[g, rows, :].astype(BF16)
                part_copy(g, back).start()

    def pair_copy(g, o):
        i = slot[o]
        return remote(
            pair_buf.at[g, pl.ds(0, T)], pair_buf.at[g, pl.ds(i * T, T)],
            pair_out.at[g, i], pair_recv.at[g, i], member(*o),
        )

    def forward_copy(g, o):
        i = slot[o]
        return remote(
            pair_buf.at[g, pl.ds(i * T, T)], pair_buf.at[g, pl.ds((i + 1) * T, T)],
            fwd_out.at[g, i], fwd_recv.at[g, i], sibling,
        )

    def own_sum(g):
        rows = pl.ds(W * T, T)
        return dk_acc[g, rows, :], dv_acc[g, rows, :]

    def send_pairs(g, own):
        dk, dv = own
        for back in range(1, W + 1):
            @pl.when(s + back < S)
            def _(back=back):
                part_copy(g, back).wait_recv()
            here = s + back < S
            got = part_in[g, back - 1]
            dk = dk + jnp.where(here, got[:, :D].astype(F32), 0.0)
            dv = dv + jnp.where(here, got[:, D:].astype(F32), 0.0)
        pair_buf[g, pl.ds(0, T), :D] = (dk * scale).astype(BF16)
        pair_buf[g, pl.ds(0, T), D:] = dv.astype(BF16)
        for o in spread[1:]:
            pair_copy(g, o).start()
        forward_copy(g, spread[0]).start()

    def forward_pairs(g):
        for o in spread[1:]:
            pair_copy(g, o).wait_recv()
            forward_copy(g, o).start()

    def rs_copy(g, h, dz):
        to = (z + dz) % NZ
        rows = pl.ds(pl.multiple_of(to * R + h * Rh, Rh), Rh)
        return remote(
            wg_half.at[g, rows], rs_in.at[g, dz - 1, pl.ds(h * Rh, Rh)],
            rs_send.at[g, h, dz - 1], rs_recv.at[g, h, dz - 1], (to * G + y, s),
        )

    def weight_part(g):
        for o in spread:
            forward_copy(g, o).wait_recv()
        total = contract(hidt_buf[...], pair_buf[g], 1, 0)
        wg_buf[g] = total
        wg_half[g] = total.astype(BF16)
        for h in range(H):
            for dz in range(1, NZ):
                rs_copy(g, h, dz).start()

    for back in range(1, W + 1):
        @pl.when(s + back >= S)
        def _(back=back):
            for g in range(KEY_VALUE_HEADS):
                part_in[g, back - 1] = jnp.zeros(part_in.shape[2:], BF16)

    pairs = per_group // 2
    middle = pairs // 2
    receive_keys(0)
    attention(0, 0, pairs)
    send_parts(0)
    receive_keys(1)
    attention(1, 0, middle)
    send_pairs(0, own_sum(0))
    attention(1, middle, pairs)
    send_parts(1)
    for o in offsets:
        hid_whole(o, hid_in.at[slot[o]]).wait()
        rows = pl.ds(slot[o] * T, T)
        hidt_buf[:, rows] = hid_buf[rows, :].T
    send_pairs(1, own_sum(1))
    forward_pairs(0)
    weight_part(0)
    forward_pairs(1)
    weight_part(1)

    width = weights_ref.shape[1]
    keep = 1.0 - learn_rate * decay_rate

    def rows_of(owner, h):
        return pl.ds(pl.multiple_of(owner * R + h * Rh, Rh), Rh)

    def up_copy(h, dc):
        rows = updated_ref.at[rows_of(s, h)]
        to = (d, ((chip + dc) % C) * 2 + core)
        return remote(rows, rows, up_out.at[h, dc], up_recv.at[h, dc], to)

    def up_forward(h, dc):
        origin = ((chip + C - dc) % C) * 2 + core
        rows = updated_ref.at[rows_of(origin, h)]
        return remote(rows, rows, upf_out.at[h, dc], upf_recv.at[h, dc], sibling)

    for h in range(H):
        grads = []
        for g in range(KEY_VALUE_HEADS):
            total = wg_buf[g, rows_of(z, h), :]
            for dz in range(1, NZ):
                rs_copy(g, h, dz).wait_recv()
                total = total + rs_in[g, dz - 1, pl.ds(h * Rh, Rh)].astype(F32)
            grads.append(total)
        square = sum(jnp.sum(t * t, axis=1, keepdims=True) for t in grads)
        factor = learn_rate / jnp.sqrt(square * (1.0 / width) + 1e-6)
        for g in range(KEY_VALUE_HEADS):
            for kind in range(2):
                columns = pl.ds((kind * KEY_VALUE_HEADS + g) * D, D)
                updated_ref[rows_of(s, h), columns] = (
                    w_vm[pl.ds(h * Rh, Rh), columns] * keep
                    - grads[g][:, kind * D : (kind + 1) * D] * factor
                ).astype(BF16)
        for dc in range(1, C):
            up_copy(h, dc).start()
        up_forward(h, 0).start()
    for h in range(H):
        for dc in range(1, C):
            up_copy(h, dc).wait_recv()
            up_forward(h, dc).start()
    for h in range(H):
        for dc in range(C):
            up_forward(h, dc).wait_recv()

    for h in range(H):
        for dc in range(C):
            if dc:
                up_copy(h, dc).wait_send()
            up_forward(h, dc).wait_send()
    for back in range(1, W + 1):
        @pl.when(s + back < S)
        def _(back=back):
            for g in range(KEY_VALUE_HEADS):
                for copy in kv_copies(g, back):
                    copy.wait_send()

        @pl.when(s >= back)
        def _(back=back):
            for g in range(KEY_VALUE_HEADS):
                part_copy(g, back).wait_send()
    for o in offsets[1:]:
        hid_whole(o, hid_out.at[slot[o]]).wait()
    for g in range(KEY_VALUE_HEADS):
        for o in spread:
            if slot[o]:
                pair_copy(g, o).wait_send()
            forward_copy(g, o).wait_send()
        for h in range(H):
            for dz in range(1, NZ):
                rs_copy(g, h, dz).wait_send()
        dq_copy(g).wait()


def body(hidden, query_states, keys, values, out_grad, seg_lengths, weights):
    S = lax.axis_size("seq")
    dp = lax.axis_size("dp")
    G = 2 if dp % 2 == 0 else 1
    NZ = dp // G
    C = S // 2
    T = hidden.shape[1]
    R, width = weights.shape
    W = S // 2
    D = HEAD_SIZE
    KV = KEY_VALUE_HEADS
    members = G * S
    strips = R % 128 == 0
    if not strips:
        hidden = hidden[0].reshape(T, NZ, G, S, R).transpose(2, 3, 0, 1, 4).reshape(members, T, NZ * R)
    H = 2 if R % 32 == 0 else 1
    plan = dict(S=S, G=G, NZ=NZ, T=T, R=R, W=W, H=H, strips=strips, ndoc=seg_lengths.shape[1])
    window = (W + 1) * T
    model = query_states.shape[2]
    dma = pltpu.SemaphoreType.DMA
    any_spec = pl.BlockSpec(memory_space=pl.ANY)
    scratch = [
        pltpu.VMEM((T, model), BF16),
        pltpu.VMEM((T, model), BF16),
        pltpu.VMEM((T, model), BF16),
        pltpu.VMEM((window, KV * D), BF16),
        pltpu.VMEM((window, KV * D), BF16),
        pltpu.VMEM((D, window), BF16),
        pltpu.VMEM((window, 2 * T), F32),
        pltpu.VMEM((KV, window, D), F32),
        pltpu.VMEM((KV, window, D), F32),
        pltpu.VMEM((KV, W, T, 2 * D), BF16),
        pltpu.VMEM((KV, W, T, 2 * D), BF16),
        pltpu.VMEM((members * T, NZ * R), BF16),
        pltpu.VMEM((NZ * R, members * T), BF16),
        pltpu.VMEM((KV, members * T, 2 * D), BF16),
        pltpu.VMEM((KV, NZ * R, 2 * D), F32),
        pltpu.VMEM((KV, NZ * R, 2 * D), BF16),
        pltpu.VMEM((KV, max(NZ - 1, 1), R, 2 * D), BF16),
        pltpu.VMEM((R, width), F32),
        dma((5,)), dma((KV,)), dma((2, KV, W)), dma((2, KV, W)), dma((members,)), dma((members,)),
        dma((KV, W)), dma((KV, W)), dma((KV, members)), dma((KV, members)),
        dma((KV, members)), dma((KV, members)),
        dma((KV, H, max(NZ - 1, 1))), dma((KV, H, max(NZ - 1, 1))),
        dma((H, C)), dma((H, C)), dma((H, C)), dma((H, C)),
    ]
    return pl.pallas_call(
        functools.partial(kernel, plan),
        out_shape=(
            jax.ShapeDtypeStruct(query_states.shape, BF16),
            jax.ShapeDtypeStruct((S * R, width), BF16),
        ),
        in_specs=[pl.BlockSpec(memory_space=pltpu.SMEM)] + [any_spec] * 6,
        out_specs=(any_spec, pl.BlockSpec(memory_space=pltpu.VMEM)),
        scratch_shapes=scratch,
        compiler_params=pltpu.CompilerParams(
            collective_id=0, has_side_effects=True, vmem_limit_bytes=56 * 1024 * 1024
        ),
    )(seg_lengths, hidden, query_states, keys, values, out_grad, weights)


def solution(mesh):
    placed = (
        P("dp", "seq", None),
        P("dp", "seq", None),
        P("dp", "seq", None),
        P("dp", "seq", None),
        P("dp", "seq", None),
        P("dp", None),
        P(("dp", "seq"), None),
    )
    return jax.shard_map(
        body,
        mesh=mesh,
        in_specs=placed,
        out_specs=(P("dp", "seq", None), P("dp", None)),
        check_vma=False,
    )
```
